32 devices in a mesh: row: 8 (over z, y), col: 4 (over x, core).
Axes of the slice: x: 2, y: 2, z: 4, core: 2. Of those that a mesh axis runs over, the one named last changes fastest.
Arguments:
- panel: float32 [131072, 256], P(('row', 'col')), may hold values from -36 to 36, as said below
Outputs:
- basis: float32 [131072, 256], P(('row', 'col'))
- factor: float32 [256, 256], replicated
The draws below stay inside these ranges and needn't reach their ends.
Inputs may be any that keep to these rules, and one draw needn't show every extreme that they name: `panel`: columns have mixed scales; entries are of order one to some tens.
All inputs are finite; a program needn't handle non-finite values.
Results may differ from the reference program's by a relative error of at most 0.0003.
Values sent between devices are 32-bit elements; how exact they have to be, the bound alone decides.
A program may use at most 128 MiB of HBM per device.

```python
import jax
import jax.numpy as jnp
from jax import lax

W = 256
ROWS = 131072


def draw_panel(key, part):
    key_vals = jax.random.fold_in(key, 11)
    key_cols = jax.random.fold_in(key, 12)
    key_common = jax.random.fold_in(key, 14)
    key_order = jax.random.fold_in(key, 15)
    order = jax.random.permutation(key_order, W).astype(jnp.float32)
    own_scale = jnp.exp(order * (jnp.log(jnp.float32(0.02)) / jnp.float32(W - 1)))[None, :]
    col_scale = jnp.exp(jax.random.uniform(key_cols, (1, W), jnp.float32, jnp.log(0.3), jnp.log(3.0)))
    common = 0.5 * jax.random.truncated_normal(key_common, -6.0, 6.0, (ROWS, 1), jnp.float32)
    values = jax.random.truncated_normal(key_vals, -6.0, 6.0, (ROWS, W), jnp.float32)
    return (common + own_scale * values) * col_scale


def setup_inputs(seed: int = 0) -> dict:
    key_list = jax.random.split(jax.random.key(seed), 2)
    return {
        "panel": draw_panel(jax.random.fold_in(key_list[1], 71), 0),
    }


def gram_of(matrix):
    return lax.dot_general(matrix.astype(jnp.float32), matrix.astype(jnp.float32), (((0,), (0,)), ((), ())), precision=lax.Precision.HIGHEST, preferred_element_type=jnp.float32)

def whiten(matrix, lower):
    return jax.scipy.linalg.solve_triangular(lower, matrix.T, lower=True).T

def reference(panel):
    lower_one = jnp.linalg.cholesky(gram_of(panel))
    first = whiten(panel, lower_one)
    lower_two = jnp.linalg.cholesky(gram_of(first))
    second = whiten(first, lower_two)
    upper = jnp.dot(lower_two.T, lower_one.T, precision=lax.Precision.HIGHEST)
    scale = jnp.sqrt(jnp.float32(ROWS))
    return (second * scale, upper / scale)
```

```python
import functools

import jax
import jax.numpy as jnp
from jax import lax
from jax.experimental import pallas as pl
from jax.experimental.pallas import tpu as pltpu
from jax.sharding import PartitionSpec as P

MESH = pl.DeviceIdType.MESH
F32 = jnp.float32
BF16 = jnp.bfloat16
VMEM_LIMIT = 48 * 1024 * 1024


def split3(value):
    high = value.astype(BF16)
    rest = value - high.astype(F32)
    mid = rest.astype(BF16)
    low = (rest - mid.astype(F32)).astype(BF16)
    return high, mid, low


def dot00(left, right):
    return lax.dot_general(left, right, (((0,), (0,)), ((), ())), preferred_element_type=F32)


def dot11(left, right):
    return lax.dot_general(left, right, (((1,), (1,)), ((), ())), preferred_element_type=F32)


def exact(left, right, dims):
    return lax.dot_general(
        left, right, (dims, ((), ())), precision=lax.Precision.HIGHEST, preferred_element_type=F32
    )


def gram_kernel(n_row, n_col, tile, a_ref, g_ref, buf, own, mixed, sum_ref, col_in, row_in, piece,
                load_sem, s1, r1, s2, r2, s3, r3, s4, r4):
    row, col = lax.axis_index("row"), lax.axis_index("col")
    rows, width = a_ref.shape
    tiles = rows // tile

    def load(step):
        return pltpu.make_async_copy(
            a_ref.at[pl.ds(step * tile, tile), :], buf.at[step], load_sem.at[step])

    for step in range(tiles):
        load(step).start()

    barrier = pltpu.get_barrier_semaphore()
    for d in range(1, n_col):
        pl.semaphore_signal(barrier, inc=1, device_id=(row, lax.rem(col + d, n_col)), device_id_type=MESH)
    for d in range(1, n_row):
        pl.semaphore_signal(barrier, inc=1, device_id=(lax.rem(row + d, n_row), col), device_id_type=MESH)

    own[...] = jnp.zeros_like(own)
    mixed[...] = jnp.zeros_like(mixed)
    for step in range(tiles):
        load(step).wait()
        high, mid, low = split3(buf[step])
        own[...] += dot00(high, high) + dot00(mid, mid)
        mixed[...] += dot00(high, mid) + dot00(high, low)
    own[...] += mixed[...] + mixed[...].T

    pl.semaphore_wait(barrier, n_col + n_row - 2)

    part = width // n_col
    copies = []
    for d in range(1, n_col):
        target = lax.rem(col + d, n_col)
        copy = pltpu.make_async_remote_copy(
            src_ref=own.at[pl.ds(pl.multiple_of(target * part, 8), part), :],
            dst_ref=col_in.at[d - 1],
            send_sem=s1.at[d - 1], recv_sem=r1.at[d - 1],
            device_id=(row, target), device_id_type=MESH)
        copy.start()
        copies.append(copy)
    total = own[pl.ds(pl.multiple_of(col * part, 8), part), :]
    for d in range(1, n_col):
        copies[d - 1].wait_recv()
        total += col_in[d - 1]
    sum_ref[...] = total
    pending = list(copies)

    if part % (8 * n_row) == 0:
        small = part // n_row
        copies = []
        for d in range(1, n_row):
            target = lax.rem(row + d, n_row)
            copy = pltpu.make_async_remote_copy(
                src_ref=sum_ref.at[pl.ds(pl.multiple_of(target * small, 8), small), :],
                dst_ref=row_in.at[d - 1],
                send_sem=s2.at[d - 1], recv_sem=r2.at[d - 1],
                device_id=(target, col), device_id_type=MESH)
            copy.start()
            copies.append(copy)
        total = sum_ref[pl.ds(pl.multiple_of(row * small, 8), small), :]
        for d in range(1, n_row):
            copies[d - 1].wait_recv()
            total += row_in[d - 1]
        piece[...] = total
        pending += copies
        mine = pl.ds(pl.multiple_of(col * part + row * small, 8), small)
        copies = []
        for d in range(1, n_row):
            copy = pltpu.make_async_remote_copy(
                src_ref=piece,
                dst_ref=g_ref.at[mine, :],
                send_sem=s3.at[d - 1], recv_sem=r3.at[d - 1],
                device_id=(lax.rem(row + d, n_row), col), device_id_type=MESH)
            copy.start()
            copies.append(copy)
        g_ref[mine, :] = total
        for copy in copies:
            copy.wait_recv()
        pending += copies
    else:
        copies = []
        for d in range(1, n_row):
            copy = pltpu.make_async_remote_copy(
                src_ref=sum_ref,
                dst_ref=row_in.at[row],
                send_sem=s2.at[d - 1], recv_sem=r2.at[d - 1],
                device_id=(lax.rem(row + d, n_row), col), device_id_type=MESH)
            copy.start()
            copies.append(copy)
        row_in[row] = total
        for copy in copies:
            copy.wait_recv()
        pending += copies
        total = row_in[0]
        for d in range(1, n_row):
            total += row_in[d]
        g_ref[pl.ds(pl.multiple_of(col * part, 8), part), :] = total

    mine = pl.ds(pl.multiple_of(col * part, 8), part)
    copies = []
    for d in range(1, n_col):
        copy = pltpu.make_async_remote_copy(
            src_ref=g_ref.at[mine, :],
            dst_ref=g_ref.at[mine, :],
            send_sem=s4.at[d - 1], recv_sem=r4.at[d - 1],
            device_id=(row, lax.rem(col + d, n_col)), device_id_type=MESH)
        copy.start()
        copies.append(copy)
    for copy in copies:
        copy.wait_recv()
    for copy in pending + copies:
        copy.wait_send()


def summed_gram(panel, collective_id):
    n_row, n_col = lax.axis_size("row"), lax.axis_size("col")
    rows, width = panel.shape
    tile = 512
    part = width // n_col
    scattered = part % (8 * n_row) == 0
    row_in = (n_row - 1, part // n_row, width) if scattered else (n_row, part, width)
    sems = []
    for count in (n_col, n_row, n_row, n_col):
        sems += [pltpu.SemaphoreType.DMA((count - 1,))] * 2
    return pl.pallas_call(
        functools.partial(gram_kernel, n_row, n_col, tile),
        out_shape=jax.ShapeDtypeStruct((width, width), F32),
        in_specs=[pl.BlockSpec(memory_space=pl.ANY)],
        out_specs=pl.BlockSpec(memory_space=pltpu.VMEM),
        scratch_shapes=[
            pltpu.VMEM((rows // tile, tile, width), F32),
            pltpu.VMEM((width, width), F32),
            pltpu.VMEM((width, width), F32),
            pltpu.VMEM((part, width), F32),
            pltpu.VMEM((n_col - 1, part, width), F32),
            pltpu.VMEM(row_in, F32),
            pltpu.VMEM((max(part // n_row, 8), width), F32),
            pltpu.SemaphoreType.DMA((rows // tile,)),
        ] + sems,
        compiler_params=pltpu.CompilerParams(
            collective_id=collective_id, has_side_effects=True, vmem_limit_bytes=VMEM_LIMIT),
        cost_estimate=pl.CostEstimate(
            flops=8 * rows * width * width, bytes_accessed=4 * rows * width, transcendentals=0),
        name="gram_sum",
    )(panel)


def eliminate(block, size):
    row_id = lax.broadcasted_iota(jnp.int32, (size, 2 * size), 0)
    col_id = lax.broadcasted_iota(jnp.int32, (size, 2 * size), 1)
    eye = (col_id == row_id + size).astype(F32)
    work = jnp.where(col_id < size, jnp.concatenate([block, block], axis=1), eye)
    scale = jnp.zeros((size, 1), F32)
    for k in range(size):
        column = work[:, k:k + 1]
        pivot_row = work[k:k + 1, :]
        pivot = work[k:k + 1, k:k + 1]
        inverse = 1.0 / pivot
        step = jnp.where(row_id[:, :1] > k, column * inverse, 0.0)
        work = work - step * pivot_row
        scale = jnp.where(row_id[:, :1] == k, pivot, scale)
    root = jnp.sqrt(scale)
    return work / root


def factor_into(g, work, upper):
    width = g.shape[0]
    size = min(64, width)
    work[...] = g[...]
    upper[...] = jnp.zeros_like(upper)
    tri_row = lax.broadcasted_iota(jnp.int32, (size, size), 0)
    tri_col = lax.broadcasted_iota(jnp.int32, (size, size), 1)
    for t in range(width // size):
        lo, hi = t * size, (t + 1) * size
        both = eliminate(work[lo:hi, lo:hi], size)
        diag = jnp.where(tri_col >= tri_row, both[:, :size], 0.0)
        inverse = jnp.where(tri_col <= tri_row, both[:, size:], 0.0)
        line = exact(inverse, work[lo:hi, :], ((1,), (0,)))
        upper[lo:hi, lo:hi] = diag
        if hi < width:
            upper[lo:hi, hi:] = line[:, hi:]
        work[lo:hi, :] = line
        work[lo:hi, lo:hi] = inverse
        if hi < width:
            work[lo:hi, lo:hi] = inverse
            work[hi:, lo:hi] = jnp.zeros((width - hi, size), F32)
            work[hi:, :] = work[hi:, :] - exact(line[:, hi:], work[lo:hi, :], ((0,), (0,)))
            work[lo:hi, hi:] = jnp.zeros((size, width - hi), F32)


def apply_kernel(total_rows, g_ref, a_ref, q_ref, factor_ref, work, upper, y_high, y_mid, y_low):
    @pl.when(pl.program_id(0) == 0)
    def _():
        factor_into(g_ref, work, upper)
        scale = jnp.sqrt(F32(total_rows))
        factor_ref[...] = upper[...] / scale
        high, mid, low = split3(work[...] * scale)
        y_high[...] = high
        y_mid[...] = mid
        y_low[...] = low

    high, mid, low = split3(a_ref[...])
    yh, ym, yl = y_high[...], y_mid[...], y_low[...]
    small = dot11(mid, ym) + dot11(high, yl) + dot11(low, yh)
    q_ref[...] = (small + dot11(high, ym) + dot11(mid, yh)) + dot11(high, yh)


def factor_and_apply(gram, panel, total_rows):
    rows, width = panel.shape
    tile = 512
    return pl.pallas_call(
        functools.partial(apply_kernel, total_rows),
        grid=(rows // tile,),
        out_shape=(
            jax.ShapeDtypeStruct((rows, width), F32),
            jax.ShapeDtypeStruct((width, width), F32),
        ),
        in_specs=[
            pl.BlockSpec((width, width), lambda i: (0, 0)),
            pl.BlockSpec((tile, width), lambda i: (i, 0)),
        ],
        out_specs=(
            pl.BlockSpec((tile, width), lambda i: (i, 0)),
            pl.BlockSpec((width, width), lambda i: (0, 0)),
        ),
        scratch_shapes=[
            pltpu.VMEM((width, width), F32),
            pltpu.VMEM((width, width), F32),
            pltpu.VMEM((width, width), BF16),
            pltpu.VMEM((width, width), BF16),
            pltpu.VMEM((width, width), BF16),
        ],
        compiler_params=pltpu.CompilerParams(vmem_limit_bytes=VMEM_LIMIT),
        cost_estimate=pl.CostEstimate(
            flops=12 * rows * width * width, bytes_accessed=8 * rows * width, transcendentals=0),
        name="factor_apply",
    )(gram, panel)


def on_device(panel):
    total_rows = panel.shape[0] * lax.axis_size("row") * lax.axis_size("col")
    gram = summed_gram(panel, 0)
    return factor_and_apply(gram, panel, total_rows)


def solution(mesh):
    return jax.shard_map(
        on_device,
        mesh=mesh,
        in_specs=(P(("row", "col"), None),),
        out_specs=(P(("row", "col"), None), P()),
        check_vma=False,
    )
```

```python
import functools

import jax
import jax.numpy as jnp
from jax import lax
from jax.experimental import pallas as pl
from jax.experimental.pallas import tpu as pltpu
from jax.sharding import PartitionSpec as P

MESH = pl.DeviceIdType.MESH
F32 = jnp.float32
BF16 = jnp.bfloat16
VMEM_LIMIT = 60 * 1024 * 1024


def split3(value):
    high = value.astype(BF16)
    rest = value - high.astype(F32)
    mid = rest.astype(BF16)
    low = (rest - mid.astype(F32)).astype(BF16)
    return high, mid, low


def dot00(left, right):
    return lax.dot_general(left, right, (((0,), (0,)), ((), ())), preferred_element_type=F32)


def dot11(left, right):
    return lax.dot_general(left, right, (((1,), (1,)), ((), ())), preferred_element_type=F32)


def exact(left, right, dims):
    return lax.dot_general(
        left, right, (dims, ((), ())), precision=lax.Precision.HIGHEST, preferred_element_type=F32
    )


def gram_kernel(near, far, n_col, tile, a_ref, g_ref, buf, own, mixed, sum_ref, col_in, row_in, piece,
                load_sem, s1, r1, s2, r2, s3, r3, s4, r4):
    row, col = lax.axis_index("row"), lax.axis_index("col")
    plane = near * n_col
    slow, fast = row // near, lax.rem(row, near)
    place = fast * n_col + col

    def in_plane(d):
        target = lax.rem(place + d, plane)
        return target, (slow * near + target // n_col, lax.rem(target, n_col))

    def across(d):
        target = lax.rem(slow + d, far)
        return target, (target * near + fast, col)

    rows, width = a_ref.shape
    tiles = rows // tile

    def load(step):
        return pltpu.make_async_copy(
            a_ref.at[pl.ds(step * tile, tile), :], buf.at[step], load_sem.at[step])

    for step in range(tiles):
        load(step).start()

    barrier = pltpu.get_barrier_semaphore()
    for d in range(1, plane):
        pl.semaphore_signal(barrier, inc=1, device_id=in_plane(d)[1], device_id_type=MESH)
    for d in range(1, far):
        pl.semaphore_signal(barrier, inc=1, device_id=across(d)[1], device_id_type=MESH)

    own[...] = jnp.zeros_like(own)
    mixed[...] = jnp.zeros_like(mixed)
    for step in range(tiles):
        load(step).wait()
        high, mid, low = split3(buf[step])
        own[...] += dot00(high, high) + dot00(mid, mid)
        mixed[...] += dot00(high, mid) + dot00(high, low)
    own[...] += mixed[...] + mixed[...].T

    pl.semaphore_wait(barrier, plane + far - 2)

    part = width // plane
    copies = []
    for d in range(1, plane):
        target, device = in_plane(d)
        copy = pltpu.make_async_remote_copy(
            src_ref=own.at[pl.ds(pl.multiple_of(target * part, 8), part), :],
            dst_ref=col_in.at[d - 1],
            send_sem=s1.at[d - 1], recv_sem=r1.at[d - 1],
            device_id=device, device_id_type=MESH)
        copy.start()
        copies.append(copy)
    total = own[pl.ds(pl.multiple_of(place * part, 8), part), :]
    for d in range(1, plane):
        copies[d - 1].wait_recv()
        total += col_in[d - 1]
    sum_ref[...] = total
    pending = list(copies)

    if part % (8 * far) == 0:
        small = part // far
        copies = []
        for d in range(1, far):
            target, device = across(d)
            copy = pltpu.make_async_remote_copy(
                src_ref=sum_ref.at[pl.ds(pl.multiple_of(target * small, 8), small), :],
                dst_ref=row_in.at[d - 1],
                send_sem=s2.at[d - 1], recv_sem=r2.at[d - 1],
                device_id=device, device_id_type=MESH)
            copy.start()
            copies.append(copy)
        total = sum_ref[pl.ds(pl.multiple_of(slow * small, 8), small), :]
        for d in range(1, far):
            copies[d - 1].wait_recv()
            total += row_in[d - 1]
        piece[...] = total
        pending += copies
        mine = pl.ds(pl.multiple_of(place * part + slow * small, 8), small)
        copies = []
        for d in range(1, far):
            copy = pltpu.make_async_remote_copy(
                src_ref=piece,
                dst_ref=g_ref.at[mine, :],
                send_sem=s3.at[d - 1], recv_sem=r3.at[d - 1],
                device_id=across(d)[1], device_id_type=MESH)
            copy.start()
            copies.append(copy)
        g_ref[mine, :] = total
        for copy in copies:
            copy.wait_recv()
        pending += copies
    else:
        copies = []
        for d in range(1, far):
            copy = pltpu.make_async_remote_copy(
                src_ref=sum_ref,
                dst_ref=row_in.at[slow],
                send_sem=s2.at[d - 1], recv_sem=r2.at[d - 1],
                device_id=across(d)[1], device_id_type=MESH)
            copy.start()
            copies.append(copy)
        row_in[slow] = total
        for copy in copies:
            copy.wait_recv()
        pending += copies
        total = row_in[0]
        for d in range(1, far):
            total += row_in[d]
        g_ref[pl.ds(pl.multiple_of(place * part, 8), part), :] = total

    mine = pl.ds(pl.multiple_of(place * part, 8), part)
    copies = []
    for d in range(1, plane):
        copy = pltpu.make_async_remote_copy(
            src_ref=g_ref.at[mine, :],
            dst_ref=g_ref.at[mine, :],
            send_sem=s4.at[d - 1], recv_sem=r4.at[d - 1],
            device_id=in_plane(d)[1], device_id_type=MESH)
        copy.start()
        copies.append(copy)
    for copy in copies:
        copy.wait_recv()
    for copy in pending + copies:
        copy.wait_send()


def summed_gram(panel, collective_id):
    n_row, n_col = lax.axis_size("row"), lax.axis_size("col")
    rows, width = panel.shape
    tile = 512
    near = 2 ** ((n_row.bit_length() - 1) // 2)
    far = n_row // near
    plane = near * n_col
    part = width // plane
    scattered = part % (8 * far) == 0
    row_in = (far - 1, part // far, width) if scattered else (far, part, width)
    sems = []
    for count in (plane, far, far, plane):
        sems += [pltpu.SemaphoreType.DMA((count - 1,))] * 2
    return pl.pallas_call(
        functools.partial(gram_kernel, near, far, n_col, tile),
        out_shape=jax.ShapeDtypeStruct((width, width), F32),
        in_specs=[pl.BlockSpec(memory_space=pl.ANY)],
        out_specs=pl.BlockSpec(memory_space=pltpu.VMEM),
        scratch_shapes=[
            pltpu.VMEM((rows // tile, tile, width), F32),
            pltpu.VMEM((width, width), F32),
            pltpu.VMEM((width, width), F32),
            pltpu.VMEM((part, width), F32),
            pltpu.VMEM((plane - 1, part, width), F32),
            pltpu.VMEM(row_in, F32),
            pltpu.VMEM((max(part // far, 8), width), F32),
            pltpu.SemaphoreType.DMA((rows // tile,)),
        ] + sems,
        compiler_params=pltpu.CompilerParams(
            collective_id=collective_id, has_side_effects=True, vmem_limit_bytes=VMEM_LIMIT),
        cost_estimate=pl.CostEstimate(
            flops=8 * rows * width * width, bytes_accessed=4 * rows * width, transcendentals=0),
        name="gram_sum",
    )(panel)


def refined_reciprocal(value):
    guess = pl.reciprocal(value, approx=True)
    guess = guess * (2.0 - value * guess)
    return guess * (2.0 - value * guess)


def eliminate(block, size):
    wide = 2 * size
    row_id = lax.broadcasted_iota(jnp.int32, (size, wide), 0)
    col_id = lax.broadcasted_iota(jnp.int32, (size, wide), 1)
    eye = (col_id == row_id + size).astype(F32)
    work = jnp.where(col_id < size, jnp.concatenate([block, block], axis=1), eye)
    tile_row = lax.broadcasted_iota(jnp.int32, (8, wide), 0)
    done = []
    for first in range(0, size, 8):
        left = size - first
        columns = [
            jnp.broadcast_to(work[:, first + j:first + j + 1], (left, wide)) for j in range(8)
        ]
        heads = [column[:8] for column in columns]
        tails = [column[8:] for column in columns]
        head, tail = work[:8], work[8:]
        pivots = jnp.zeros((8, wide), F32)
        for k in range(8):
            pivot = jnp.broadcast_to(heads[k][k:k + 1], (8, wide))
            inverse = refined_reciprocal(pivot)
            pivots = jnp.where(tile_row == k, pivot, pivots)
            line = head[k:k + 1] * inverse[:1]
            step = jnp.where(tile_row > k, heads[k], 0.0)
            head = head - step * line
            if left > 8:
                tail = tail - tails[k] * line
            for j in range(k + 1, 8):
                ratio = heads[j][k:k + 1] * inverse[:1]
                if left > 8:
                    tails[j] = tails[j] - tails[k] * ratio
                heads[j] = heads[j] - step * ratio
        done.append(head / jnp.sqrt(pivots))
        work = tail
    return jnp.concatenate(done, axis=0)


def factor_into(g, work, upper):
    width = g.shape[0]
    size = min(64, width)
    work[...] = g[...]
    upper[...] = jnp.zeros_like(upper)
    tri_row = lax.broadcasted_iota(jnp.int32, (size, size), 0)
    tri_col = lax.broadcasted_iota(jnp.int32, (size, size), 1)
    for t in range(width // size):
        lo, hi = t * size, (t + 1) * size
        both = eliminate(work[lo:hi, lo:hi], size)
        diag = jnp.where(tri_col >= tri_row, both[:, :size], 0.0)
        inverse = jnp.where(tri_col <= tri_row, both[:, size:], 0.0)
        line = exact(inverse, work[lo:hi, :], ((1,), (0,)))
        upper[lo:hi, lo:hi] = diag
        if hi < width:
            upper[lo:hi, hi:] = line[:, hi:]
        work[lo:hi, :] = line
        work[lo:hi, lo:hi] = inverse
        if hi < width:
            work[lo:hi, lo:hi] = inverse
            work[hi:, lo:hi] = jnp.zeros((width - hi, size), F32)
            work[hi:, :] = work[hi:, :] - exact(line[:, hi:], work[lo:hi, :], ((0,), (0,)))
            work[lo:hi, hi:] = jnp.zeros((size, width - hi), F32)


def apply_kernel(total_rows, g_ref, a_ref, q_ref, factor_ref, work, upper, y_high, y_mid, y_low):
    @pl.when(pl.program_id(0) == 0)
    def _():
        factor_into(g_ref, work, upper)
        scale = jnp.sqrt(F32(total_rows))
        factor_ref[...] = upper[...] / scale
        high, mid, low = split3(work[...] * scale)
        y_high[...] = high
        y_mid[...] = mid
        y_low[...] = low

    high, mid, low = split3(a_ref[...])
    yh, ym, yl = y_high[...], y_mid[...], y_low[...]
    small = dot11(mid, ym) + dot11(high, yl) + dot11(low, yh)
    q_ref[...] = (small + dot11(high, ym) + dot11(mid, yh)) + dot11(high, yh)


def factor_and_apply(gram, panel, total_rows):
    rows, width = panel.shape
    tile = 512
    return pl.pallas_call(
        functools.partial(apply_kernel, total_rows),
        grid=(rows // tile,),
        out_shape=(
            jax.ShapeDtypeStruct((rows, width), F32),
            jax.ShapeDtypeStruct((width, width), F32),
        ),
        in_specs=[
            pl.BlockSpec((width, width), lambda i: (0, 0)),
            pl.BlockSpec((tile, width), lambda i: (i, 0)),
        ],
        out_specs=(
            pl.BlockSpec((tile, width), lambda i: (i, 0)),
            pl.BlockSpec((width, width), lambda i: (0, 0)),
        ),
        scratch_shapes=[
            pltpu.VMEM((width, width), F32),
            pltpu.VMEM((width, width), F32),
            pltpu.VMEM((width, width), BF16),
            pltpu.VMEM((width, width), BF16),
            pltpu.VMEM((width, width), BF16),
        ],
        compiler_params=pltpu.CompilerParams(vmem_limit_bytes=VMEM_LIMIT),
        cost_estimate=pl.CostEstimate(
            flops=12 * rows * width * width, bytes_accessed=8 * rows * width, transcendentals=0),
        name="factor_apply",
    )(gram, panel)


def on_device(panel):
    total_rows = panel.shape[0] * lax.axis_size("row") * lax.axis_size("col")
    gram = summed_gram(panel, 0)
    return factor_and_apply(gram, panel, total_rows)


def solution(mesh):
    return jax.shard_map(
        on_device,
        mesh=mesh,
        in_specs=(P(("row", "col"), None),),
        out_specs=(P(("row", "col"), None), P()),
        check_vma=False,
    )
```

```python
import functools

import jax
import jax.numpy as jnp
from jax import lax
from jax.experimental import pallas as pl
from jax.experimental.pallas import tpu as pltpu
from jax.sharding import PartitionSpec as P

MESH = pl.DeviceIdType.MESH
F32 = jnp.float32
BF16 = jnp.bfloat16
VMEM_LIMIT = 60 * 1024 * 1024


def split3(value):
    high = value.astype(BF16)
    rest = value - high.astype(F32)
    mid = rest.astype(BF16)
    low = (rest - mid.astype(F32)).astype(BF16)
    return high, mid, low


def dot00(left, right):
    return lax.dot_general(left, right, (((0,), (0,)), ((), ())), preferred_element_type=F32)


def dot11(left, right):
    return lax.dot_general(left, right, (((1,), (1,)), ((), ())), preferred_element_type=F32)


def exact(left, right, dims):
    return lax.dot_general(
        left, right, (dims, ((), ())), precision=lax.Precision.HIGHEST, preferred_element_type=F32
    )


def gram_kernel(near, far, n_col, tile, a_ref, g_ref, buf, own, mixed, sum_ref, col_in, row_in,
                load_sem, s1, r1, s2, r2, s4, r4):
    row, col = lax.axis_index("row"), lax.axis_index("col")
    plane = near * n_col
    slow, fast = row // near, lax.rem(row, near)
    place = fast * n_col + col

    def in_plane(d):
        target = lax.rem(place + d, plane)
        return target, (slow * near + target // n_col, lax.rem(target, n_col))

    def across(d):
        target = lax.rem(slow + d, far)
        return target, (target * near + fast, col)

    rows, width = a_ref.shape
    tiles = rows // tile

    def load(step):
        return pltpu.make_async_copy(
            a_ref.at[pl.ds(step * tile, tile), :], buf.at[step], load_sem.at[step])

    for step in range(tiles):
        load(step).start()

    barrier = pltpu.get_barrier_semaphore()
    for d in range(1, plane):
        pl.semaphore_signal(barrier, inc=1, device_id=in_plane(d)[1], device_id_type=MESH)
    for d in range(1, far):
        pl.semaphore_signal(barrier, inc=1, device_id=across(d)[1], device_id_type=MESH)

    own[...] = jnp.zeros_like(own)
    mixed[...] = jnp.zeros_like(mixed)
    for step in range(tiles):
        load(step).wait()
        high, mid, low = split3(buf[step])
        own[...] += dot00(high, high) + dot00(mid, mid)
        mixed[...] += dot00(high, mid) + dot00(high, low)
    whole = own[...] + (mixed[...] + mixed[...].T)
    if g_ref.shape[0] < width:
        half, quarter = width // 2, width // 4
        own[:half, :] = whole[:half, :]
        own[half:half + quarter, :half] = whole[half:half + quarter, half:]
        own[half:half + quarter, half:] = whole[half + quarter:, half:]
    else:
        own[...] = whole

    pl.semaphore_wait(barrier, plane + far - 2)

    part = g_ref.shape[0] // plane
    copies = []
    for d in range(1, plane):
        target, device = in_plane(d)
        copy = pltpu.make_async_remote_copy(
            src_ref=own.at[pl.ds(pl.multiple_of(target * part, 8), part), :],
            dst_ref=col_in.at[d - 1],
            send_sem=s1.at[d - 1], recv_sem=r1.at[d - 1],
            device_id=device, device_id_type=MESH)
        copy.start()
        copies.append(copy)
    total = own[pl.ds(pl.multiple_of(place * part, 8), part), :]
    for d in range(1, plane):
        copies[d - 1].wait_recv()
        total += col_in[d - 1]
    sum_ref[...] = total
    pending = list(copies)

    copies = []
    for d in range(1, far):
        copy = pltpu.make_async_remote_copy(
            src_ref=sum_ref,
            dst_ref=row_in.at[slow],
            send_sem=s2.at[d - 1], recv_sem=r2.at[d - 1],
            device_id=across(d)[1], device_id_type=MESH)
        copy.start()
        copies.append(copy)
    row_in[slow] = total
    for copy in copies:
        copy.wait_recv()
    pending += copies
    total = row_in[0]
    for d in range(1, far):
        total += row_in[d]
    g_ref[pl.ds(pl.multiple_of(place * part, 8), part), :] = total

    mine = pl.ds(pl.multiple_of(place * part, 8), part)
    copies = []
    for d in range(1, plane):
        copy = pltpu.make_async_remote_copy(
            src_ref=g_ref.at[mine, :],
            dst_ref=g_ref.at[mine, :],
            send_sem=s4.at[d - 1], recv_sem=r4.at[d - 1],
            device_id=in_plane(d)[1], device_id_type=MESH)
        copy.start()
        copies.append(copy)
    for copy in copies:
        copy.wait_recv()
    for copy in pending + copies:
        copy.wait_send()


def summed_gram(panel, collective_id):
    n_row, n_col = lax.axis_size("row"), lax.axis_size("col")
    rows, width = panel.shape
    tile = 512
    near = 2 ** ((n_row.bit_length() - 1) // 2)
    far = n_row // near
    plane = near * n_col
    packed = 3 * width // 4
    if packed % (8 * plane) or width % 256:
        packed = width
    part = packed // plane
    sems = []
    for count in (plane, far, plane):
        sems += [pltpu.SemaphoreType.DMA((count - 1,))] * 2
    return pl.pallas_call(
        functools.partial(gram_kernel, near, far, n_col, tile),
        out_shape=jax.ShapeDtypeStruct((packed, width), F32),
        in_specs=[pl.BlockSpec(memory_space=pl.ANY)],
        out_specs=pl.BlockSpec(memory_space=pltpu.VMEM),
        scratch_shapes=[
            pltpu.VMEM((rows // tile, tile, width), F32),
            pltpu.VMEM((width, width), F32),
            pltpu.VMEM((width, width), F32),
            pltpu.VMEM((part, width), F32),
            pltpu.VMEM((plane - 1, part, width), F32),
            pltpu.VMEM((far, part, width), F32),
            pltpu.SemaphoreType.DMA((rows // tile,)),
        ] + sems,
        compiler_params=pltpu.CompilerParams(
            collective_id=collective_id, has_side_effects=True, vmem_limit_bytes=VMEM_LIMIT),
        cost_estimate=pl.CostEstimate(
            flops=8 * rows * width * width, bytes_accessed=4 * rows * width, transcendentals=0),
        name="gram_sum",
    )(panel)


def refined_reciprocal(value):
    guess = pl.reciprocal(value, approx=True)
    guess = guess * (2.0 - value * guess)
    return guess * (2.0 - value * guess)


def eliminate(block, size):
    wide = 2 * size
    row_id = lax.broadcasted_iota(jnp.int32, (size, wide), 0)
    col_id = lax.broadcasted_iota(jnp.int32, (size, wide), 1)
    eye = (col_id == row_id + size).astype(F32)
    work = jnp.where(col_id < size, jnp.concatenate([block, block], axis=1), eye)
    tile_row = lax.broadcasted_iota(jnp.int32, (8, wide), 0)
    done = []
    for first in range(0, size, 8):
        left = size - first
        columns = [
            jnp.broadcast_to(work[:, first + j:first + j + 1], (left, wide)) for j in range(8)
        ]
        heads = [column[:8] for column in columns]
        tails = [column[8:] for column in columns]
        head, tail = work[:8], work[8:]
        pivots = jnp.zeros((8, wide), F32)
        for k in range(8):
            pivot = jnp.broadcast_to(heads[k][k:k + 1], (8, wide))
            inverse = refined_reciprocal(pivot)
            pivots = jnp.where(tile_row == k, pivot, pivots)
            line = head[k:k + 1] * inverse[:1]
            step = jnp.where(tile_row > k, heads[k], 0.0)
            head = head - step * line
            if left > 8:
                tail = tail - tails[k] * line
            for j in range(k + 1, 8):
                ratio = heads[j][k:k + 1] * inverse[:1]
                if left > 8:
                    tails[j] = tails[j] - tails[k] * ratio
                heads[j] = heads[j] - step * ratio
        done.append(head / jnp.sqrt(pivots))
        work = tail
    return jnp.concatenate(done, axis=0)


def factor_into(g, work, upper):
    width = g.shape[1]
    size = min(64, width)
    if g.shape[0] < width:
        half, quarter = width // 2, width // 4
        work[:half, :] = g[:half, :]
        work[half:, :half] = jnp.zeros((half, half), F32)
        work[half:half + quarter, half:] = g[half:, :half]
        work[half + quarter:, half:] = g[half:, half:]
    else:
        work[...] = g[...]
    upper[...] = jnp.zeros_like(upper)
    tri_row = lax.broadcasted_iota(jnp.int32, (size, size), 0)
    tri_col = lax.broadcasted_iota(jnp.int32, (size, size), 1)
    for t in range(width // size):
        lo, hi = t * size, (t + 1) * size
        both = eliminate(work[lo:hi, lo:hi], size)
        diag = jnp.where(tri_col >= tri_row, both[:, :size], 0.0)
        inverse = jnp.where(tri_col <= tri_row, both[:, size:], 0.0)
        line = exact(inverse, work[lo:hi, :], ((1,), (0,)))
        upper[lo:hi, lo:hi] = diag
        if hi < width:
            upper[lo:hi, hi:] = line[:, hi:]
        work[lo:hi, :] = line
        work[lo:hi, lo:hi] = inverse
        if hi < width:
            work[lo:hi, lo:hi] = inverse
            work[hi:, lo:hi] = jnp.zeros((width - hi, size), F32)
            work[hi:, :] = work[hi:, :] - exact(line[:, hi:], work[lo:hi, :], ((0,), (0,)))
            work[lo:hi, hi:] = jnp.zeros((size, width - hi), F32)


def apply_kernel(total_rows, tile, g_ref, a_ref, q_ref, factor_ref, work, upper, a_buf, q_buf, in_sem, out_sem):
    tiles = a_ref.shape[0] // tile

    def load(step):
        return pltpu.make_async_copy(
            a_ref.at[pl.ds(step * tile, tile), :], a_buf.at[step], in_sem.at[step])

    def store(step):
        return pltpu.make_async_copy(
            q_buf.at[step], q_ref.at[pl.ds(step * tile, tile), :], out_sem.at[step])

    for step in range(tiles):
        load(step).start()
    factor_into(g_ref, work, upper)
    scale = jnp.sqrt(F32(total_rows))
    factor_ref[...] = upper[...] / scale
    y_high, y_mid, _ = split3(work[...] * scale)
    for step in range(tiles):
        load(step).wait()
        high, mid, _ = split3(a_buf[step])
        q_buf[step] = (dot11(high, y_mid) + dot11(mid, y_high)) + dot11(high, y_high)
        store(step).start()
    for step in range(tiles):
        store(step).wait()


def factor_and_apply(gram, panel, total_rows):
    rows, width = panel.shape
    tile = 512
    tiles = rows // tile
    return pl.pallas_call(
        functools.partial(apply_kernel, total_rows, tile),
        out_shape=(
            jax.ShapeDtypeStruct((rows, width), F32),
            jax.ShapeDtypeStruct((width, width), F32),
        ),
        in_specs=[
            pl.BlockSpec(memory_space=pltpu.VMEM),
            pl.BlockSpec(memory_space=pl.ANY),
        ],
        out_specs=(
            pl.BlockSpec(memory_space=pl.ANY),
            pl.BlockSpec(memory_space=pltpu.VMEM),
        ),
        scratch_shapes=[
            pltpu.VMEM((width, width), F32),
            pltpu.VMEM((width, width), F32),
            pltpu.VMEM((tiles, tile, width), F32),
            pltpu.VMEM((tiles, tile, width), F32),
            pltpu.SemaphoreType.DMA((tiles,)),
            pltpu.SemaphoreType.DMA((tiles,)),
        ],
        compiler_params=pltpu.CompilerParams(vmem_limit_bytes=VMEM_LIMIT),
        cost_estimate=pl.CostEstimate(
            flops=6 * rows * width * width, bytes_accessed=8 * rows * width, transcendentals=0),
        name="factor_apply",
    )(gram, panel)


def on_device(panel):
    total_rows = panel.shape[0] * lax.axis_size("row") * lax.axis_size("col")
    gram = summed_gram(panel, 0)
    return factor_and_apply(gram, panel, total_rows)


def solution(mesh):
    return jax.shard_map(
        on_device,
        mesh=mesh,
        in_specs=(P(("row", "col"), None),),
        out_specs=(P(("row", "col"), None), P()),
        check_vma=False,
    )
```

```python
import functools

import jax
import jax.numpy as jnp
from jax import lax
from jax.experimental import pallas as pl
from jax.experimental.pallas import tpu as pltpu
from jax.sharding import PartitionSpec as P

MESH = pl.DeviceIdType.MESH
F32 = jnp.float32
BF16 = jnp.bfloat16
VMEM_LIMIT = 60 * 1024 * 1024


def split3(value):
    high = value.astype(BF16)
    rest = value - high.astype(F32)
    mid = rest.astype(BF16)
    low = (rest - mid.astype(F32)).astype(BF16)
    return high, mid, low


def dot00(left, right):
    return lax.dot_general(left, right, (((0,), (0,)), ((), ())), preferred_element_type=F32)


def dot11(left, right):
    return lax.dot_general(left, right, (((1,), (1,)), ((), ())), preferred_element_type=F32)


def exact(left, right, dims):
    return lax.dot_general(
        left, right, (dims, ((), ())), precision=lax.Precision.HIGHEST, preferred_element_type=F32
    )


def gram_kernel(near, far, n_col, tile, a_ref, g_ref, buf, own, mixed, sum_ref, col_in, row_in,
                load_sem, s1, r1, s2, r2, s4, r4):
    row, col = lax.axis_index("row"), lax.axis_index("col")
    plane = near * n_col
    slow, fast = row // near, lax.rem(row, near)
    place = fast * n_col + col

    def in_plane(d):
        target = lax.rem(place + d, plane)
        return target, (slow * near + target // n_col, lax.rem(target, n_col))

    def across(d):
        target = lax.rem(slow + d, far)
        return target, (target * near + fast, col)

    rows, width = a_ref.shape
    tiles = rows // tile

    def load(step):
        return pltpu.make_async_copy(
            a_ref.at[pl.ds(step * tile, tile), :], buf.at[step], load_sem.at[step])

    for step in range(tiles):
        load(step).start()

    barrier = pltpu.get_barrier_semaphore()
    for d in range(1, plane):
        pl.semaphore_signal(barrier, inc=1, device_id=in_plane(d)[1], device_id_type=MESH)
    for d in range(1, far):
        pl.semaphore_signal(barrier, inc=1, device_id=across(d)[1], device_id_type=MESH)

    own[...] = jnp.zeros_like(own)
    mixed[...] = jnp.zeros_like(mixed)
    for step in range(tiles):
        load(step).wait()
        high, mid, low = split3(buf[step])
        own[...] += dot00(high, high) + dot00(mid, mid)
        mixed[...] += dot00(high, mid) + dot00(high, low)
    whole = own[...] + (mixed[...] + mixed[...].T)
    if g_ref.shape[0] < width:
        half, quarter = width // 2, width // 4
        own[:half, :] = whole[:half, :]
        own[half:half + quarter, :half] = whole[half:half + quarter, half:]
        own[half:half + quarter, half:] = whole[half + quarter:, half:]
    else:
        own[...] = whole

    pl.semaphore_wait(barrier, plane + far - 2)

    part = g_ref.shape[0] // plane
    copies = []
    for d in range(1, plane):
        target, device = in_plane(d)
        copy = pltpu.make_async_remote_copy(
            src_ref=own.at[pl.ds(pl.multiple_of(target * part, 8), part), :],
            dst_ref=col_in.at[d - 1],
            send_sem=s1.at[d - 1], recv_sem=r1.at[d - 1],
            device_id=device, device_id_type=MESH)
        copy.start()
        copies.append(copy)
    total = own[pl.ds(pl.multiple_of(place * part, 8), part), :]
    for d in range(1, plane):
        copies[d - 1].wait_recv()
        total += col_in[d - 1]
    sum_ref[...] = total
    pending = list(copies)

    copies = []
    for d in range(1, far):
        copy = pltpu.make_async_remote_copy(
            src_ref=sum_ref,
            dst_ref=row_in.at[slow],
            send_sem=s2.at[d - 1], recv_sem=r2.at[d - 1],
            device_id=across(d)[1], device_id_type=MESH)
        copy.start()
        copies.append(copy)
    row_in[slow] = total
    for copy in copies:
        copy.wait_recv()
    pending += copies
    total = row_in[0]
    for d in range(1, far):
        total += row_in[d]
    g_ref[pl.ds(pl.multiple_of(place * part, 8), part), :] = total

    mine = pl.ds(pl.multiple_of(place * part, 8), part)
    copies = []
    for d in range(1, plane):
        copy = pltpu.make_async_remote_copy(
            src_ref=g_ref.at[mine, :],
            dst_ref=g_ref.at[mine, :],
            send_sem=s4.at[d - 1], recv_sem=r4.at[d - 1],
            device_id=in_plane(d)[1], device_id_type=MESH)
        copy.start()
        copies.append(copy)
    for copy in copies:
        copy.wait_recv()
    for copy in pending + copies:
        copy.wait_send()


def summed_gram(panel, collective_id):
    n_row, n_col = lax.axis_size("row"), lax.axis_size("col")
    rows, width = panel.shape
    tile = 512
    near = 2 ** ((n_row.bit_length() - 1) // 2)
    far = n_row // near
    plane = near * n_col
    packed = 3 * width // 4
    if packed % (8 * plane) or width % 256:
        packed = width
    part = packed // plane
    sems = []
    for count in (plane, far, plane):
        sems += [pltpu.SemaphoreType.DMA((count - 1,))] * 2
    return pl.pallas_call(
        functools.partial(gram_kernel, near, far, n_col, tile),
        out_shape=jax.ShapeDtypeStruct((packed, width), F32),
        in_specs=[pl.BlockSpec(memory_space=pl.ANY)],
        out_specs=pl.BlockSpec(memory_space=pltpu.VMEM),
        scratch_shapes=[
            pltpu.VMEM((rows // tile, tile, width), F32),
            pltpu.VMEM((width, width), F32),
            pltpu.VMEM((width, width), F32),
            pltpu.VMEM((part, width), F32),
            pltpu.VMEM((plane - 1, part, width), F32),
            pltpu.VMEM((far, part, width), F32),
            pltpu.SemaphoreType.DMA((rows // tile,)),
        ] + sems,
        compiler_params=pltpu.CompilerParams(
            collective_id=collective_id, has_side_effects=True, vmem_limit_bytes=VMEM_LIMIT),
        cost_estimate=pl.CostEstimate(
            flops=8 * rows * width * width, bytes_accessed=4 * rows * width, transcendentals=0),
        name="gram_sum",
    )(panel)


def eliminate(block, size, between):
    wide = 2 * size
    row_id = lax.broadcasted_iota(jnp.int32, (size, wide), 0)
    col_id = lax.broadcasted_iota(jnp.int32, (size, wide), 1)
    eye = (col_id == row_id + size).astype(F32)
    work = jnp.where(col_id < size, jnp.concatenate([block, block], axis=1), eye)
    tile_row = lax.broadcasted_iota(jnp.int32, (8, wide), 0)
    done = []
    for first in range(0, size, 8):
        left = size - first
        columns = [
            jnp.broadcast_to(work[:, first + j:first + j + 1], (left, wide)) for j in range(8)
        ]
        heads = [column[:8] for column in columns]
        tails = [[column[i:i + 8] for i in range(8, left, 8)] for column in columns]
        head, tail = work[:8], [work[i:i + 8] for i in range(8, left, 8)]
        pivots = jnp.ones((8, wide), F32)
        for k in range(8):
            rows = [jnp.broadcast_to(heads[j][k:k + 1], (8, wide)) for j in range(k, 8)]
            line = jnp.broadcast_to(head[k:k + 1], (8, wide))
            inverse = pl.reciprocal(rows[0], approx=True)
            pivots = jnp.where(tile_row == k, rows[0], pivots)
            step = jnp.where(tile_row > k, heads[k], 0.0)
            for j in range(k + 1, 8):
                heads[j] = heads[j] - (step * rows[j - k]) * inverse
            head = head - (step * line) * inverse
            scaled_line = line * inverse
            scaled_rows = [row * inverse for row in rows]
            for i in range(len(tail)):
                tail[i] = tail[i] - tails[k][i] * scaled_line
                for j in range(k + 1, 8):
                    tails[j][i] = tails[j][i] - tails[k][i] * scaled_rows[j - k]
        done.append(head / jnp.sqrt(pivots))
        if tail:
            work = jnp.concatenate(tail, axis=0)
        if between:
            between[first // 8]()
    return jnp.concatenate(done, axis=0)


def factor_into(g, work, upper, before, between):
    width = g.shape[1]
    size = min(64, width)
    if g.shape[0] < width:
        half, quarter = width // 2, width // 4
        work[:half, :] = g[:half, :]
        work[half:, :half] = jnp.zeros((half, half), F32)
        work[half:half + quarter, half:] = g[half:, :half]
        work[half + quarter:, half:] = g[half:, half:]
    else:
        work[...] = g[...]
    upper[...] = jnp.zeros_like(upper)
    tri_row = lax.broadcasted_iota(jnp.int32, (size, size), 0)
    tri_col = lax.broadcasted_iota(jnp.int32, (size, size), 1)
    for t in range(width // size):
        lo, hi = t * size, (t + 1) * size
        if t in before:
            before[t]()
        both = eliminate(work[lo:hi, lo:hi], size, between.get(t))
        diag = jnp.where(tri_col >= tri_row, both[:, :size], 0.0)
        inverse = jnp.where(tri_col <= tri_row, both[:, size:], 0.0)
        line = exact(inverse, work[lo:hi, :], ((1,), (0,)))
        upper[lo:hi, lo:hi] = diag
        if hi < width:
            upper[lo:hi, hi:] = line[:, hi:]
        work[lo:hi, :] = line
        work[lo:hi, lo:hi] = inverse
        if hi < width:
            work[lo:hi, lo:hi] = inverse
            work[hi:, lo:hi] = jnp.zeros((width - hi, size), F32)
            work[hi:, :] = work[hi:, :] - exact(line[:, hi:], work[lo:hi, :], ((0,), (0,)))
            work[lo:hi, hi:] = jnp.zeros((size, width - hi), F32)


def apply_kernel(total_rows, tile, g_ref, a_ref, q_ref, factor_ref, work, upper, a_buf, a_high, a_mid,
                 y_wide, q_buf, in_sem, out_sem):
    rows, width = a_ref.shape
    tiles, half = rows // tile, width // 2
    scale = jnp.sqrt(F32(total_rows))

    def load(step):
        return pltpu.make_async_copy(
            a_ref.at[pl.ds(step * tile, tile), :], a_buf.at[step], in_sem.at[step])

    def store(step, side):
        return pltpu.make_async_copy(
            q_buf.at[step, :, pl.ds(side * half, half)],
            q_ref.at[pl.ds(step * tile, tile), pl.ds(side * half, half)],
            out_sem.at[side, step])

    def loaded():
        for step in range(tiles):
            load(step).wait()

    def split(step):
        a_high[step], a_mid[step], _ = split3(a_buf[step])

    def prepare(side):
        depth = (side + 1) * half
        y = (work[side * half:depth, :depth] * scale).T
        y_wide[:depth, :half], y_wide[:depth, half:], _ = split3(y)

    def columns(side, step):
        depth = (side + 1) * half
        both = jnp.dot(a_high[step, :, :depth], y_wide[:depth, :], preferred_element_type=F32)
        cross = jnp.dot(a_mid[step, :, :depth], y_wide[:depth, :half], preferred_element_type=F32)
        q_buf[step, :, side * half:depth] = both[:, :half] + (both[:, half:] + cross)

    def first_out():
        for step in range(tiles):
            store(step, 0).start()

    for step in range(tiles):
        load(step).start()
    before = {1: loaded, 2: functools.partial(prepare, 0), 3: first_out}
    between = {
        1: [functools.partial(split, step) for step in range(tiles)],
        2: [functools.partial(columns, 0, step) for step in range(tiles)],
    }
    factor_into(g_ref, work, upper, before, between)
    prepare(1)
    for step in range(tiles):
        columns(1, step)
        store(step, 1).start()
    factor_ref[...] = upper[...] / scale
    for side in range(2):
        for step in range(tiles):
            store(step, side).wait()


def factor_and_apply(gram, panel, total_rows):
    rows, width = panel.shape
    tiles = 8
    tile = rows // tiles
    return pl.pallas_call(
        functools.partial(apply_kernel, total_rows, tile),
        out_shape=(
            jax.ShapeDtypeStruct((rows, width), F32),
            jax.ShapeDtypeStruct((width, width), F32),
        ),
        in_specs=[
            pl.BlockSpec(memory_space=pltpu.VMEM),
            pl.BlockSpec(memory_space=pl.ANY),
        ],
        out_specs=(
            pl.BlockSpec(memory_space=pl.ANY),
            pl.BlockSpec(memory_space=pltpu.VMEM),
        ),
        scratch_shapes=[
            pltpu.VMEM((width, width), F32),
            pltpu.VMEM((width, width), F32),
            pltpu.VMEM((tiles, tile, width), F32),
            pltpu.VMEM((tiles, tile, width), BF16),
            pltpu.VMEM((tiles, tile, width), BF16),
            pltpu.VMEM((width, width), BF16),
            pltpu.VMEM((tiles, tile, width), F32),
            pltpu.SemaphoreType.DMA((tiles,)),
            pltpu.SemaphoreType.DMA((2, tiles)),
        ],
        compiler_params=pltpu.CompilerParams(vmem_limit_bytes=VMEM_LIMIT),
        cost_estimate=pl.CostEstimate(
            flops=6 * rows * width * width, bytes_accessed=8 * rows * width, transcendentals=0),
        name="factor_apply",
    )(gram, panel)


def on_device(panel):
    total_rows = panel.shape[0] * lax.axis_size("row") * lax.axis_size("col")
    gram = summed_gram(panel, 0)
    return factor_and_apply(gram, panel, total_rows)


def solution(mesh):
    return jax.shard_map(
        on_device,
        mesh=mesh,
        in_specs=(P(("row", "col"), None),),
        out_specs=(P(("row", "col"), None), P()),
        check_vma=False,
    )
```

```python
import functools

import jax
import jax.numpy as jnp
from jax import lax
from jax.experimental import pallas as pl
from jax.experimental.pallas import tpu as pltpu
from jax.sharding import PartitionSpec as P

MESH = pl.DeviceIdType.MESH
F32 = jnp.float32
BF16 = jnp.bfloat16
VMEM_LIMIT = 60 * 1024 * 1024


def split3(value):
    high = value.astype(BF16)
    rest = value - high.astype(F32)
    mid = rest.astype(BF16)
    low = (rest - mid.astype(F32)).astype(BF16)
    return high, mid, low


def dot00(left, right):
    return lax.dot_general(left, right, (((0,), (0,)), ((), ())), preferred_element_type=F32)


def dot11(left, right):
    return lax.dot_general(left, right, (((1,), (1,)), ((), ())), preferred_element_type=F32)


def exact(left, right, dims):
    return lax.dot_general(
        left, right, (dims, ((), ())), precision=lax.Precision.HIGHEST, preferred_element_type=F32
    )


def gram_kernel(near, far, n_col, tile, a_ref, g_ref, buf, own, mixed, sum_ref, col_in, row_in,
                load_sem, s1, r1, s2, r2, s4, r4):
    row, col = lax.axis_index("row"), lax.axis_index("col")
    plane = near * n_col
    slow, fast = row // near, lax.rem(row, near)
    place = fast * n_col + col

    def in_plane(d):
        target = lax.rem(place + d, plane)
        return target, (slow * near + target // n_col, lax.rem(target, n_col))

    def across(d):
        target = lax.rem(slow + d, far)
        return target, (target * near + fast, col)

    rows, width = a_ref.shape
    tiles = rows // tile

    def load(step):
        return pltpu.make_async_copy(
            a_ref.at[pl.ds(step * tile, tile), :], buf.at[step], load_sem.at[step])

    for step in range(tiles):
        load(step).start()

    barrier = pltpu.get_barrier_semaphore()
    for d in range(1, plane):
        pl.semaphore_signal(barrier, inc=1, device_id=in_plane(d)[1], device_id_type=MESH)
    for d in range(1, far):
        pl.semaphore_signal(barrier, inc=1, device_id=across(d)[1], device_id_type=MESH)

    own[...] = jnp.zeros_like(own)
    mixed[...] = jnp.zeros_like(mixed)
    for step in range(tiles):
        load(step).wait()
        high, mid, low = split3(buf[step])
        own[...] += dot00(high, high) + dot00(mid, mid)
        mixed[...] += dot00(high, mid) + dot00(high, low)
    whole = own[...] + (mixed[...] + mixed[...].T)
    if g_ref.shape[0] < width:
        half, quarter = width // 2, width // 4
        own[:half, :] = whole[:half, :]
        own[half:half + quarter, :half] = whole[half:half + quarter, half:]
        own[half:half + quarter, half:] = whole[half + quarter:, half:]
    else:
        own[...] = whole

    pl.semaphore_wait(barrier, plane + far - 2)

    part = g_ref.shape[0] // plane
    half = width // 2
    mine = pl.ds(pl.multiple_of(place * part, 8), part)
    lanes = [pl.ds(0, half), pl.ds(half, half)]

    def scatter(side, d):
        target, device = in_plane(d)
        return pltpu.make_async_remote_copy(
            src_ref=own.at[pl.ds(pl.multiple_of(target * part, 8), part), lanes[side]],
            dst_ref=col_in.at[side, d - 1],
            send_sem=s1.at[side, d - 1], recv_sem=r1.at[side, d - 1],
            device_id=device, device_id_type=MESH)

    def exchange(side, d):
        return pltpu.make_async_remote_copy(
            src_ref=sum_ref.at[side],
            dst_ref=row_in.at[side, slow],
            send_sem=s2.at[side, d - 1], recv_sem=r2.at[side, d - 1],
            device_id=across(d)[1], device_id_type=MESH)

    def gather(side, d):
        return pltpu.make_async_remote_copy(
            src_ref=g_ref.at[mine, lanes[side]],
            dst_ref=g_ref.at[mine, lanes[side]],
            send_sem=s4.at[side, d - 1], recv_sem=r4.at[side, d - 1],
            device_id=in_plane(d)[1], device_id_type=MESH)

    def start(make, side, count):
        copies = [make(side, d) for d in range(1, count)]
        for copy in copies:
            copy.start()
        return copies

    scattered = [start(scatter, side, plane) for side in range(2)]
    exchanged, gathered = [], []
    for side in range(2):
        total = own[mine, lanes[side]]
        for d in range(1, plane):
            scattered[side][d - 1].wait_recv()
            total += col_in[side, d - 1]
        sum_ref[side] = total
        exchanged.append(start(exchange, side, far))
        row_in[side, slow] = total
    for side in range(2):
        for copy in exchanged[side]:
            copy.wait_recv()
        total = row_in[side, 0]
        for d in range(1, far):
            total += row_in[side, d]
        g_ref[mine, lanes[side]] = total
        gathered.append(start(gather, side, plane))
    for side in range(2):
        for copy in gathered[side]:
            copy.wait_recv()
    for side in range(2):
        for copy in scattered[side] + exchanged[side] + gathered[side]:
            copy.wait_send()


def summed_gram(panel, collective_id):
    n_row, n_col = lax.axis_size("row"), lax.axis_size("col")
    rows, width = panel.shape
    tile = 512
    near = 2 ** ((n_row.bit_length() - 1) // 2)
    far = n_row // near
    plane = near * n_col
    packed = 3 * width // 4
    if packed % (8 * plane) or width % 256:
        packed = width
    part = packed // plane
    sems = []
    for count in (plane, far, plane):
        sems += [pltpu.SemaphoreType.DMA((2, count - 1))] * 2
    return pl.pallas_call(
        functools.partial(gram_kernel, near, far, n_col, tile),
        out_shape=jax.ShapeDtypeStruct((packed, width), F32),
        in_specs=[pl.BlockSpec(memory_space=pl.ANY)],
        out_specs=pl.BlockSpec(memory_space=pltpu.VMEM),
        scratch_shapes=[
            pltpu.VMEM((rows // tile, tile, width), F32),
            pltpu.VMEM((width, width), F32),
            pltpu.VMEM((width, width), F32),
            pltpu.VMEM((2, part, width // 2), F32),
            pltpu.VMEM((2, plane - 1, part, width // 2), F32),
            pltpu.VMEM((2, far, part, width // 2), F32),
            pltpu.SemaphoreType.DMA((rows // tile,)),
        ] + sems,
        compiler_params=pltpu.CompilerParams(
            collective_id=collective_id, has_side_effects=True, vmem_limit_bytes=VMEM_LIMIT),
        cost_estimate=pl.CostEstimate(
            flops=8 * rows * width * width, bytes_accessed=4 * rows * width, transcendentals=0),
        name="gram_sum",
    )(panel)


def eliminate(block, size, between):
    wide = 2 * size
    row_id = lax.broadcasted_iota(jnp.int32, (size, wide), 0)
    col_id = lax.broadcasted_iota(jnp.int32, (size, wide), 1)
    eye = (col_id == row_id + size).astype(F32)
    work = jnp.where(col_id < size, jnp.concatenate([block, block], axis=1), eye)
    tile_row = lax.broadcasted_iota(jnp.int32, (8, wide), 0)
    done = []
    for first in range(0, size, 8):
        left = size - first
        columns = [
            jnp.broadcast_to(work[:, first + j:first + j + 1], (left, wide)) for j in range(8)
        ]
        heads = [column[:8] for column in columns]
        tails = [[column[i:i + 8] for i in range(8, left, 8)] for column in columns]
        head, tail = work[:8], [work[i:i + 8] for i in range(8, left, 8)]
        pivots = jnp.ones((8, wide), F32)
        for k in range(8):
            rows = [jnp.broadcast_to(heads[j][k:k + 1], (8, wide)) for j in range(k, 8)]
            line = jnp.broadcast_to(head[k:k + 1], (8, wide))
            inverse = pl.reciprocal(rows[0], approx=True)
            pivots = jnp.where(tile_row == k, rows[0], pivots)
            step = jnp.where(tile_row > k, heads[k], 0.0)
            for j in range(k + 1, 8):
                heads[j] = heads[j] - (step * rows[j - k]) * inverse
            head = head - (step * line) * inverse
            scaled_line = line * inverse
            scaled_rows = [row * inverse for row in rows]
            for i in range(len(tail)):
                tail[i] = tail[i] - tails[k][i] * scaled_line
                for j in range(k + 1, 8):
                    tails[j][i] = tails[j][i] - tails[k][i] * scaled_rows[j - k]
        done.append(head / jnp.sqrt(pivots))
        if tail:
            work = jnp.concatenate(tail, axis=0)
        if between:
            between[first // 8]()
    return jnp.concatenate(done, axis=0)


def factor_into(g, work, upper, before, between):
    width = g.shape[1]
    size = min(64, width)
    if g.shape[0] < width:
        half, quarter = width // 2, width // 4
        work[:half, :] = g[:half, :]
        work[half:, :half] = jnp.zeros((half, half), F32)
        work[half:half + quarter, half:] = g[half:, :half]
        work[half + quarter:, half:] = g[half:, half:]
    else:
        work[...] = g[...]
    upper[...] = jnp.zeros_like(upper)
    tri_row = lax.broadcasted_iota(jnp.int32, (size, size), 0)
    tri_col = lax.broadcasted_iota(jnp.int32, (size, size), 1)
    for t in range(width // size):
        lo, hi = t * size, (t + 1) * size
        if t in before:
            before[t]()
        both = eliminate(work[lo:hi, lo:hi], size, between.get(t))
        diag = jnp.where(tri_col >= tri_row, both[:, :size], 0.0)
        inverse = jnp.where(tri_col <= tri_row, both[:, size:], 0.0)
        line = exact(inverse, work[lo:hi, :], ((1,), (0,)))
        upper[lo:hi, lo:hi] = diag
        if hi < width:
            upper[lo:hi, hi:] = line[:, hi:]
        work[lo:hi, :] = line
        work[lo:hi, lo:hi] = inverse
        if hi < width:
            work[lo:hi, lo:hi] = inverse
            work[hi:, lo:hi] = jnp.zeros((width - hi, size), F32)
            work[hi:, :] = work[hi:, :] - exact(line[:, hi:], work[lo:hi, :], ((0,), (0,)))
            work[lo:hi, hi:] = jnp.zeros((size, width - hi), F32)


def apply_kernel(total_rows, tile, g_ref, a_ref, q_ref, factor_ref, work, upper, a_buf, a_high, a_mid,
                 y_wide, q_buf, in_sem, out_sem):
    rows, width = a_ref.shape
    tiles, half = rows // tile, width // 2
    scale = jnp.sqrt(F32(total_rows))

    def load(step):
        return pltpu.make_async_copy(
            a_ref.at[pl.ds(step * tile, tile), :], a_buf.at[step], in_sem.at[step])

    def store(step, side):
        return pltpu.make_async_copy(
            q_buf.at[step, :, pl.ds(side * half, half)],
            q_ref.at[pl.ds(step * tile, tile), pl.ds(side * half, half)],
            out_sem.at[side, step])

    def loaded():
        for step in range(tiles):
            load(step).wait()

    def split(step):
        a_high[step], a_mid[step], _ = split3(a_buf[step])

    def prepare(side):
        depth = (side + 1) * half
        y = (work[side * half:depth, :depth] * scale).T
        y_wide[:depth, :half], y_wide[:depth, half:], _ = split3(y)

    def columns(side, step):
        depth = (side + 1) * half
        both = jnp.dot(a_high[step, :, :depth], y_wide[:depth, :], preferred_element_type=F32)
        cross = jnp.dot(a_mid[step, :, :depth], y_wide[:depth, :half], preferred_element_type=F32)
        q_buf[step, :, side * half:depth] = both[:, :half] + (both[:, half:] + cross)

    def first_out():
        for step in range(tiles):
            store(step, 0).start()

    for step in range(tiles):
        load(step).start()
    before = {1: loaded, 2: functools.partial(prepare, 0), 3: first_out}
    between = {
        1: [functools.partial(split, step) for step in range(tiles)],
        2: [functools.partial(columns, 0, step) for step in range(tiles)],
    }
    factor_into(g_ref, work, upper, before, between)
    prepare(1)
    for step in range(tiles):
        columns(1, step)
        store(step, 1).start()
    factor_ref[...] = upper[...] / scale
    for side in range(2):
        for step in range(tiles):
            store(step, side).wait()


def factor_and_apply(gram, panel, total_rows):
    rows, width = panel.shape
    tiles = 8
    tile = rows // tiles
    return pl.pallas_call(
        functools.partial(apply_kernel, total_rows, tile),
        out_shape=(
            jax.ShapeDtypeStruct((rows, width), F32),
            jax.ShapeDtypeStruct((width, width), F32),
        ),
        in_specs=[
            pl.BlockSpec(memory_space=pltpu.VMEM),
            pl.BlockSpec(memory_space=pl.ANY),
        ],
        out_specs=(
            pl.BlockSpec(memory_space=pl.ANY),
            pl.BlockSpec(memory_space=pltpu.VMEM),
        ),
        scratch_shapes=[
            pltpu.VMEM((width, width), F32),
            pltpu.VMEM((width, width), F32),
            pltpu.VMEM((tiles, tile, width), F32),
            pltpu.VMEM((tiles, tile, width), BF16),
            pltpu.VMEM((tiles, tile, width), BF16),
            pltpu.VMEM((width, width), BF16),
            pltpu.VMEM((tiles, tile, width), F32),
            pltpu.SemaphoreType.DMA((tiles,)),
            pltpu.SemaphoreType.DMA((2, tiles)),
        ],
        compiler_params=pltpu.CompilerParams(vmem_limit_bytes=VMEM_LIMIT),
        cost_estimate=pl.CostEstimate(
            flops=6 * rows * width * width, bytes_accessed=8 * rows * width, transcendentals=0),
        name="factor_apply",
    )(gram, panel)


def on_device(panel):
    total_rows = panel.shape[0] * lax.axis_size("row") * lax.axis_size("col")
    gram = summed_gram(panel, 0)
    return factor_and_apply(gram, panel, total_rows)


def solution(mesh):
    return jax.shard_map(
        on_device,
        mesh=mesh,
        in_specs=(P(("row", "col"), None),),
        out_specs=(P(("row", "col"), None), P()),
        check_vma=False,
    )
```

```python
import functools

import jax
import jax.numpy as jnp
from jax import lax
from jax.experimental import pallas as pl
from jax.experimental.pallas import tpu as pltpu
from jax.sharding import PartitionSpec as P

MESH = pl.DeviceIdType.MESH
F32 = jnp.float32
BF16 = jnp.bfloat16
VMEM_LIMIT = 60 * 1024 * 1024


def split3(value):
    high = value.astype(BF16)
    rest = value - high.astype(F32)
    mid = rest.astype(BF16)
    low = (rest - mid.astype(F32)).astype(BF16)
    return high, mid, low


def dot00(left, right):
    return lax.dot_general(left, right, (((0,), (0,)), ((), ())), preferred_element_type=F32)


def dot11(left, right):
    return lax.dot_general(left, right, (((1,), (1,)), ((), ())), preferred_element_type=F32)


def exact(left, right, dims):
    return lax.dot_general(
        left, right, (dims, ((), ())), precision=lax.Precision.HIGHEST, preferred_element_type=F32
    )


def gram_kernel(near, far, n_col, tile, a_ref, g_ref, buf, own, mixed, sum_ref, col_in, row_in,
                load_sem, s1, r1, s2, r2, s4, r4):
    row, col = lax.axis_index("row"), lax.axis_index("col")
    plane = near * n_col
    slow, fast = row // near, lax.rem(row, near)
    place = fast * n_col + col

    def in_plane(d):
        target = lax.rem(place + d, plane)
        return target, (slow * near + target // n_col, lax.rem(target, n_col))

    def across(d):
        target = lax.rem(slow + d, far)
        return target, (target * near + fast, col)

    rows, width = a_ref.shape
    tiles = rows // tile

    def load(step):
        return pltpu.make_async_copy(
            a_ref.at[pl.ds(step * tile, tile), :], buf.at[step], load_sem.at[step])

    for step in range(tiles):
        load(step).start()

    barrier = pltpu.get_barrier_semaphore()
    for d in range(1, plane):
        pl.semaphore_signal(barrier, inc=1, device_id=in_plane(d)[1], device_id_type=MESH)
    for d in range(1, far):
        pl.semaphore_signal(barrier, inc=1, device_id=across(d)[1], device_id_type=MESH)

    own[...] = jnp.zeros_like(own)
    mixed[...] = jnp.zeros_like(mixed)
    for step in range(tiles):
        load(step).wait()
        high, mid, low = split3(buf[step])
        own[...] += dot00(high, high) + dot00(mid, mid)
        mixed[...] += dot00(high, mid) + dot00(high, low)
    whole = own[...] + (mixed[...] + mixed[...].T)
    if g_ref.shape[0] < width:
        half, quarter = width // 2, width // 4
        own[:half, :] = whole[:half, :]
        own[half:half + quarter, :half] = whole[half:half + quarter, half:]
        own[half:half + quarter, half:] = whole[half + quarter:, half:]
    else:
        own[...] = whole

    pl.semaphore_wait(barrier, plane + far - 2)

    part = g_ref.shape[0] // plane
    copies = []
    for d in range(1, plane):
        target, device = in_plane(d)
        copy = pltpu.make_async_remote_copy(
            src_ref=own.at[pl.ds(pl.multiple_of(target * part, 8), part), :],
            dst_ref=col_in.at[d - 1],
            send_sem=s1.at[d - 1], recv_sem=r1.at[d - 1],
            device_id=device, device_id_type=MESH)
        copy.start()
        copies.append(copy)
    total = own[pl.ds(pl.multiple_of(place * part, 8), part), :]
    for d in range(1, plane):
        copies[d - 1].wait_recv()
        total += col_in[d - 1]
    sum_ref[...] = total
    pending = list(copies)

    copies = []
    for d in range(1, far):
        copy = pltpu.make_async_remote_copy(
            src_ref=sum_ref,
            dst_ref=row_in.at[slow],
            send_sem=s2.at[d - 1], recv_sem=r2.at[d - 1],
            device_id=across(d)[1], device_id_type=MESH)
        copy.start()
        copies.append(copy)
    row_in[slow] = total
    for copy in copies:
        copy.wait_recv()
    pending += copies
    total = row_in[0]
    for d in range(1, far):
        total += row_in[d]
    g_ref[pl.ds(pl.multiple_of(place * part, 8), part), :] = total

    mine = pl.ds(pl.multiple_of(place * part, 8), part)
    copies = []
    for d in range(1, plane):
        copy = pltpu.make_async_remote_copy(
            src_ref=g_ref.at[mine, :],
            dst_ref=g_ref.at[mine, :],
            send_sem=s4.at[d - 1], recv_sem=r4.at[d - 1],
            device_id=in_plane(d)[1], device_id_type=MESH)
        copy.start()
        copies.append(copy)
    for copy in copies:
        copy.wait_recv()
    for copy in pending + copies:
        copy.wait_send()


def summed_gram(panel, collective_id):
    n_row, n_col = lax.axis_size("row"), lax.axis_size("col")
    rows, width = panel.shape
    tile = 1024
    near = 2 ** ((n_row.bit_length() - 1) // 2)
    far = n_row // near
    plane = near * n_col
    packed = 3 * width // 4
    if packed % (8 * plane) or width % 256:
        packed = width
    part = packed // plane
    sems = []
    for count in (plane, far, plane):
        sems += [pltpu.SemaphoreType.DMA((count - 1,))] * 2
    return pl.pallas_call(
        functools.partial(gram_kernel, near, far, n_col, tile),
        out_shape=jax.ShapeDtypeStruct((packed, width), F32),
        in_specs=[pl.BlockSpec(memory_space=pl.ANY)],
        out_specs=pl.BlockSpec(memory_space=pltpu.VMEM),
        scratch_shapes=[
            pltpu.VMEM((rows // tile, tile, width), F32),
            pltpu.VMEM((width, width), F32),
            pltpu.VMEM((width, width), F32),
            pltpu.VMEM((part, width), F32),
            pltpu.VMEM((plane - 1, part, width), F32),
            pltpu.VMEM((far, part, width), F32),
            pltpu.SemaphoreType.DMA((rows // tile,)),
        ] + sems,
        compiler_params=pltpu.CompilerParams(
            collective_id=collective_id, has_side_effects=True, vmem_limit_bytes=VMEM_LIMIT),
        cost_estimate=pl.CostEstimate(
            flops=8 * rows * width * width, bytes_accessed=4 * rows * width, transcendentals=0),
        name="gram_sum",
    )(panel)


def eliminate(block, size, between):
    wide = 2 * size
    row_id = lax.broadcasted_iota(jnp.int32, (size, wide), 0)
    col_id = lax.broadcasted_iota(jnp.int32, (size, wide), 1)
    eye = (col_id == row_id + size).astype(F32)
    work = jnp.where(col_id < size, jnp.concatenate([block, block], axis=1), eye)
    tile_row = lax.broadcasted_iota(jnp.int32, (8, wide), 0)
    done = []
    for first in range(0, size, 8):
        left = size - first
        columns = [
            jnp.broadcast_to(work[:, first + j:first + j + 1], (left, wide)) for j in range(8)
        ]
        heads = [column[:8] for column in columns]
        tails = [[column[i:i + 8] for i in range(8, left, 8)] for column in columns]
        head, tail = work[:8], [work[i:i + 8] for i in range(8, left, 8)]
        pivots = jnp.ones((8, wide), F32)
        for k in range(8):
            rows = [jnp.broadcast_to(heads[j][k:k + 1], (8, wide)) for j in range(k, 8)]
            line = jnp.broadcast_to(head[k:k + 1], (8, wide))
            inverse = pl.reciprocal(rows[0], approx=True)
            pivots = jnp.where(tile_row == k, rows[0], pivots)
            step = jnp.where(tile_row > k, heads[k], 0.0)
            for j in range(k + 1, 8):
                heads[j] = heads[j] - (step * rows[j - k]) * inverse
            head = head - (step * line) * inverse
            scaled_line = line * inverse
            scaled_rows = [row * inverse for row in rows]
            for i in range(len(tail)):
                tail[i] = tail[i] - tails[k][i] * scaled_line
                for j in range(k + 1, 8):
                    tails[j][i] = tails[j][i] - tails[k][i] * scaled_rows[j - k]
        done.append(head / jnp.sqrt(pivots))
        if tail:
            work = jnp.concatenate(tail, axis=0)
        if between:
            between[first // 8]()
    return jnp.concatenate(done, axis=0)


def factor_into(g, work, upper, before, between):
    width = g.shape[1]
    size = min(64, width)
    if g.shape[0] < width:
        half, quarter = width // 2, width // 4
        work[:half, :] = g[:half, :]
        work[half:, :half] = jnp.zeros((half, half), F32)
        work[half:half + quarter, half:] = g[half:, :half]
        work[half + quarter:, half:] = g[half:, half:]
    else:
        work[...] = g[...]
    upper[...] = jnp.zeros_like(upper)
    tri_row = lax.broadcasted_iota(jnp.int32, (size, size), 0)
    tri_col = lax.broadcasted_iota(jnp.int32, (size, size), 1)
    for t in range(width // size):
        lo, hi = t * size, (t + 1) * size
        if t in before:
            before[t]()
        both = eliminate(work[lo:hi, lo:hi], size, between.get(t))
        diag = jnp.where(tri_col >= tri_row, both[:, :size], 0.0)
        inverse = jnp.where(tri_col <= tri_row, both[:, size:], 0.0)
        line = exact(inverse, work[lo:hi, :], ((1,), (0,)))
        upper[lo:hi, lo:hi] = diag
        if hi < width:
            upper[lo:hi, hi:] = line[:, hi:]
        work[lo:hi, :] = line
        work[lo:hi, lo:hi] = inverse
        if hi < width:
            work[lo:hi, lo:hi] = inverse
            work[hi:, lo:hi] = jnp.zeros((width - hi, size), F32)
            work[hi:, :] = work[hi:, :] - exact(line[:, hi:], work[lo:hi, :], ((0,), (0,)))
            work[lo:hi, hi:] = jnp.zeros((size, width - hi), F32)


def apply_kernel(total_rows, tile, g_ref, a_ref, q_ref, factor_ref, work, upper, a_buf, a_high, a_mid,
                 y_wide, q_buf, in_sem, out_sem, factor_sem):
    rows, width = a_ref.shape
    tiles, half = rows // tile, width // 2
    scale = jnp.sqrt(F32(total_rows))

    def load(step):
        return pltpu.make_async_copy(
            a_ref.at[pl.ds(step * tile, tile), :], a_buf.at[step], in_sem.at[step])

    def store(step, side):
        return pltpu.make_async_copy(
            q_buf.at[step, :, pl.ds(side * half, half)],
            q_ref.at[pl.ds(step * tile, tile), pl.ds(side * half, half)],
            out_sem.at[side, step])

    def loaded():
        for step in range(tiles):
            load(step).wait()

    def split(step):
        a_high[step], a_mid[step], _ = split3(a_buf[step])

    def prepare(side):
        depth = (side + 1) * half
        y = (work[side * half:depth, :depth] * scale).T
        y_wide[:depth, :half], y_wide[:depth, half:], _ = split3(y)

    def columns(side, step):
        depth = (side + 1) * half
        both = jnp.dot(a_high[step, :, :depth], y_wide[:depth, :], preferred_element_type=F32)
        cross = jnp.dot(a_mid[step, :, :depth], y_wide[:depth, :half], preferred_element_type=F32)
        q_buf[step, :, side * half:depth] = both[:, :half] + (both[:, half:] + cross)

    def first_out():
        for step in range(tiles):
            store(step, 0).start()

    for step in range(tiles):
        load(step).start()
    before = {1: loaded, 2: functools.partial(prepare, 0), 3: first_out}
    between = {
        1: [functools.partial(split, step) for step in range(tiles)],
        2: [functools.partial(columns, 0, step) for step in range(tiles)],
    }
    factor_into(g_ref, work, upper, before, between)
    prepare(1)
    upper[...] = upper[...] / scale
    factor_out = pltpu.make_async_copy(upper, factor_ref, factor_sem)
    factor_out.start()
    for step in range(tiles):
        columns(1, step)
        store(step, 1).start()
    factor_out.wait()
    for side in range(2):
        for step in range(tiles):
            store(step, side).wait()


def factor_and_apply(gram, panel, total_rows):
    rows, width = panel.shape
    tiles = 8
    tile = rows // tiles
    return pl.pallas_call(
        functools.partial(apply_kernel, total_rows, tile),
        out_shape=(
            jax.ShapeDtypeStruct((rows, width), F32),
            jax.ShapeDtypeStruct((width, width), F32),
        ),
        in_specs=[
            pl.BlockSpec(memory_space=pltpu.VMEM),
            pl.BlockSpec(memory_space=pl.ANY),
        ],
        out_specs=(
            pl.BlockSpec(memory_space=pl.ANY),
            pl.BlockSpec(memory_space=pl.ANY),
        ),
        scratch_shapes=[
            pltpu.VMEM((width, width), F32),
            pltpu.VMEM((width, width), F32),
            pltpu.VMEM((tiles, tile, width), F32),
            pltpu.VMEM((tiles, tile, width), BF16),
            pltpu.VMEM((tiles, tile, width), BF16),
            pltpu.VMEM((width, width), BF16),
            pltpu.VMEM((tiles, tile, width), F32),
            pltpu.SemaphoreType.DMA((tiles,)),
            pltpu.SemaphoreType.DMA((2, tiles)),
            pltpu.SemaphoreType.DMA,
        ],
        compiler_params=pltpu.CompilerParams(vmem_limit_bytes=VMEM_LIMIT),
        cost_estimate=pl.CostEstimate(
            flops=6 * rows * width * width, bytes_accessed=8 * rows * width, transcendentals=0),
        name="factor_apply",
    )(gram, panel)


def on_device(panel):
    total_rows = panel.shape[0] * lax.axis_size("row") * lax.axis_size("col")
    gram = summed_gram(panel, 0)
    return factor_and_apply(gram, panel, total_rows)


def solution(mesh):
    return jax.shard_map(
        on_device,
        mesh=mesh,
        in_specs=(P(("row", "col"), None),),
        out_specs=(P(("row", "col"), None), P()),
        check_vma=False,
    )
```
